32 devices in a mesh: groups: 2 (over y), ctx: 4 (over z), tp: 4 (over x, core).
Axes of the slice: x: 2, y: 2, z: 4, core: 2. Of those that a mesh axis runs over, the one named last changes fastest.
Arguments:
- queries: bfloat16 [1024, 8192], P(('groups', 'ctx'), 'tp'), parts along dimension 0, may hold values from -5 to 5
- suffix_keys_values: bfloat16 [2, 1024, 1024], P(None, ('groups', 'ctx'), 'tp'), parts along dimension 1, may hold values from -5 to 5
- cached_page_pool: bfloat16 [2, 256, 16, 1024], P(None, ('groups', 'ctx'), None, 'tp'), parts along dimension 1, may hold values from -5 to 5
- prefix_page_hits: int32 [8, 32], P('groups'), parts along dimension 0, may hold values from 0 to 127, as said below
- lengths: int32 [8], P('groups'), parts along dimension 0, may hold values from 1 to 256, 512 in all
- mamba_x: bfloat16 [1024, 8192], P(('groups', 'ctx'), 'tp'), parts along dimension 0, may hold values from -5 to 5
- gate_z: bfloat16 [1024, 8192], P(('groups', 'ctx'), 'tp'), parts along dimension 0, may hold values from -6 to 6
- delta: bfloat16 [1024, 8192], P(('groups', 'ctx'), 'tp'), parts along dimension 0, may hold values from -7 to 1.024
- b_c: float32 [2, 16, 1024], P(None, None, ('groups', 'ctx')), parts along dimension 2, may hold values from -5 to 5
- a_log: float32 [16, 8192], P(None, 'tp'), may hold values from -6 to 4
- d_skip: float32 [8192], P('tp'), may hold values from 0.5 to 1.5
- state_pool: float32 [16, 16, 8192], P(('groups', 'ctx'), None, 'tp'), parts along dimension 0, may hold values from -3 to 3
- state_hits: int32 [8], P('groups'), parts along dimension 0, may hold values from 0 to 7, as said below
Outputs:
- attention_out: bfloat16 [1024, 8192], P(('groups', 'ctx'), 'tp'), parts along dimension 0
- mamba_out: bfloat16 [1024, 8192], P(('groups', 'ctx'), 'tp'), parts along dimension 0
The draws below stay inside these ranges and needn't reach their ends.
There are 2 independent parts, one for each index of `groups`. The reference program is written for one: setup_inputs(seed, part) draws one part's arguments, and reference() takes and returns one part's arrays. A program takes and returns all parts, laid end to end along the dimension named above; an argument that names none is the same for every part. Nothing has to cross between parts.
Inputs may be any that keep to these rules, and one draw needn't show every extreme that they name: `prefix_page_hits`: page p is held by ctx device p // 32; a request's 32 pages are distinct, requests may share pages. `state_hits`: slot s is held by ctx device s // 2; requests have distinct slots.
All inputs are finite; a program needn't handle non-finite values.
Results may differ from the reference program's by a relative error of at most 0.007.
Values may be sent and summed in bfloat16 or wider, within the bound.
A program may use at most 128 MiB of HBM per device.

```python
import math
import jax
import jax.numpy as jnp
import numpy as np
from jax import lax

ASKING_HEADCOUNT = 64
MEMORY_HEADCOUNT = 8
PER_HEAD_DIM = 128
STATE_FEATURES = 8192
NS = 16
R = 4
PAGE_TOKENS = 16
NHIT = 32
TAIL_ENTRY_TOTAL = 512
POOL_PAGES = 128
SLOTS = 8
MAXIMAL_TAIL = 256


def draw_queries(key, part):
    key = jax.random.fold_in(key, 11)
    reference_answer = jnp.clip(jax.random.normal(key, (TAIL_ENTRY_TOTAL, ASKING_HEADCOUNT * PER_HEAD_DIM), jnp.float32), -4.0, 4.0)
    return reference_answer.astype(jnp.bfloat16)


def draw_suffix_keys_values(key, part):
    key = jax.random.fold_in(key, 12)
    key_portion, value_portion = jax.random.split(key, 2)
    address_line_indices = jnp.clip(jax.random.normal(key_portion, (TAIL_ENTRY_TOTAL, MEMORY_HEADCOUNT * PER_HEAD_DIM), jnp.float32), -4.0, 4.0)
    value_row_list = jnp.clip(jax.random.normal(value_portion, (TAIL_ENTRY_TOTAL, MEMORY_HEADCOUNT * PER_HEAD_DIM), jnp.float32), -4.0, 4.0)
    return jnp.stack([address_line_indices, value_row_list]).astype(jnp.bfloat16)


def draw_prefix_page_hits(key, part):
    key = jax.random.fold_in(key, 15)
    request_keys = jax.random.split(key, R)
    chosen = jax.vmap(lambda single: jax.random.permutation(single, POOL_PAGES)[:NHIT])(request_keys)
    return chosen.astype(jnp.int32)


def draw_state_hits(key, part):
    key = jax.random.fold_in(key, 16)
    return jax.random.permutation(key, SLOTS)[:R].astype(jnp.int32)


def draw_delta(key, part):
    key = jax.random.fold_in(key, 13)
    base_key, location_seed, magnitude_seed = jax.random.split(key, 3)
    reference_answer = -5.5 + 0.5 * jnp.clip(jax.random.normal(base_key, (TAIL_ENTRY_TOTAL, STATE_FEATURES), jnp.float32), -3.0, 3.0)
    spike_positions = jax.random.randint(location_seed, (4,), 0, TAIL_ENTRY_TOTAL)
    spike_line_indices = jnp.any(jnp.arange(TAIL_ENTRY_TOTAL)[:, None] == spike_positions[None, :], axis=1)[:, None]
    spike_spacing = jax.random.uniform(magnitude_seed, (TAIL_ENTRY_TOTAL, STATE_FEATURES), jnp.float32, 0.0015, 0.004) * MAXIMAL_TAIL
    spike_samples = spike_spacing + jnp.log(-jnp.expm1(-spike_spacing))
    return jnp.where(spike_line_indices, spike_samples, reference_answer).astype(jnp.bfloat16)


def draw_a_log(key, part):
    key = jax.random.fold_in(key, 14)
    class_key, slow_key, fast_key, spread_key = jax.random.split(key, 4)
    slow_mask = jax.random.randint(class_key, (1, STATE_FEATURES), 0, 10) < 5
    slow_rate = jnp.exp(jax.random.uniform(slow_key, (1, STATE_FEATURES), jnp.float32, math.log(0.3), math.log(1.2))) / (0.004 * MAXIMAL_TAIL)
    fast_rate = jnp.exp(jax.random.uniform(fast_key, (1, STATE_FEATURES), jnp.float32, math.log(4.0), math.log(8.0)))
    spread = jnp.exp(jax.random.uniform(spread_key, (NS, STATE_FEATURES), jnp.float32, math.log(0.7), math.log(1.4)))
    return jnp.log(jnp.where(slow_mask, slow_rate, fast_rate) * spread)


def block_levels(own_key, shape, shards, low, top_value):
    def one(position, parts):
        steps = jax.random.uniform(jax.random.fold_in(jax.random.fold_in(own_key, 6), position), (parts,), jnp.float32, low / len(shards), top_value / len(shards))
        return jnp.repeat(jnp.exp(steps), shape[position] // parts).reshape((-1,) + (1,) * (len(shape) - position - 1))

    gain = one(*shards[0])
    for cut in shards[1:]:
        gain = gain * one(*cut)
    return gain


def length_profile(count, total, reach, slope):
    portions = [(1 << 20) // math.isqrt(standing ** slope) + 1 for standing in range(2, count + 1)]
    spare, counts = total - reach - (count - 1), [1] * (count - 1)
    while spare > 0:
        candidates = [i for i in range(count - 1) if counts[i] < reach]
        mass, left = sum([portions[i] for i in candidates]), spare
        for i in candidates:
            addition = min(reach - counts[i], max(1, left * portions[i] // mass), spare)
            counts[i] = counts[i] + addition
            spare = spare - addition
    return np.array([reach] + counts)


def uneven(own_key, number_of, total, bound, slope):
    if number_of == 2:
        one = jax.random.randint(own_key, (), max(1, total - bound), min(bound, total - 1) + 1)
        return jnp.stack([one, total - one])
    tallies = jnp.asarray(length_profile(number_of, total, bound, slope), jnp.int32)
    couples = (number_of - 1) // 2
    giver, taker = tallies[1:1 + 2 * couples:2], tallies[2:2 + 2 * couples:2]
    margin = jnp.minimum(giver - 1, bound - taker)
    passed = jax.random.randint(jax.random.fold_in(own_key, 1), (couples,), 0, 1 << 20) % (margin + 1)
    tallies = tallies.at[1:1 + 2 * couples:2].set(giver - passed).at[2:2 + 2 * couples:2].set(taker + passed)
    return tallies[jax.random.permutation(jax.random.fold_in(own_key, 2), number_of)]


def noise(rng, dims, width, limit, shards=(), held_as=jnp.bfloat16):
    array = jax.random.normal(rng, dims, jnp.float32) * width
    if len(shards) > 0:
        array = block_levels(rng, dims, shards, -0.22, 0.18) * array
    return jnp.clip(array, min=-limit, max=limit).astype(held_as)


def setup_inputs(seed: int = 0, part: int = 0) -> dict:
    key_of = jax.random.split(jax.random.key(seed), 14)
    own_keys = jax.random.split(jax.random.fold_in(key_of[13], part), 14)
    queries = draw_queries(jax.random.fold_in(jax.random.fold_in(key_of[13], part), 71), part)
    suffix_keys_values = draw_suffix_keys_values(jax.random.fold_in(jax.random.fold_in(key_of[13], part), 71), part)
    cached_page_pool = noise(own_keys[2], (2, POOL_PAGES, PAGE_TOKENS, MEMORY_HEADCOUNT * PER_HEAD_DIM), 1.0, 5.0, ((1, 4), (3, 4)))
    prefix_page_hits = draw_prefix_page_hits(jax.random.fold_in(jax.random.fold_in(key_of[13], part), 71), part)
    lengths = uneven(own_keys[4], R, TAIL_ENTRY_TOTAL, MAXIMAL_TAIL, 2).astype(jnp.int32)
    mamba_x = noise(own_keys[5], (TAIL_ENTRY_TOTAL, STATE_FEATURES), 1.0, 5.0, ((0, 4), (1, 4)))
    gate_z = noise(own_keys[6], (TAIL_ENTRY_TOTAL, STATE_FEATURES), 1.5, 6.0, ((0, 4), (1, 4)))
    delta = draw_delta(jax.random.fold_in(jax.random.fold_in(key_of[13], part), 71), part)
    b_c = noise(own_keys[8], (2, NS, TAIL_ENTRY_TOTAL), 1.0, 5.0, ((2, 4),), jnp.float32)
    a_log = draw_a_log(jax.random.fold_in(key_of[13], 71), part)
    d_skip = jnp.clip(0.5 + 1.0 * jax.random.uniform(key_of[10], (STATE_FEATURES,), jnp.float32) ** block_levels(key_of[10], (STATE_FEATURES,), ((0, 4),), -0.2, 0.2), 0.5, 1.5)
    state_pool = noise(own_keys[11], (SLOTS, NS, STATE_FEATURES), 0.5, 3.0, ((0, 4), (2, 4)), jnp.float32)
    state_hits = draw_state_hits(jax.random.fold_in(jax.random.fold_in(key_of[13], part), 71), part)
    return {"queries": queries, "suffix_keys_values": suffix_keys_values, "cached_page_pool": cached_page_pool, "prefix_page_hits": prefix_page_hits, "lengths": lengths, "mamba_x": mamba_x, "gate_z": gate_z, "delta": delta, "b_c": b_c, "a_log": a_log, "d_skip": d_skip, "state_pool": state_pool, "state_hits": state_hits}


FLOOR_SCORE = -1e+30

def segments_of(positions, lengths):
    ends = jnp.cumsum(lengths)
    starts = ends - lengths
    member = (positions[:, None] >= starts[None, :]).astype(jnp.int32)
    return (lax.optimization_barrier(jnp.sum(member, axis=1)) - 1, starts)

def attention_part(queries, suffix_keys_values, cached_page_pool, prefix_page_hits, positions, segment):
    group_share = ASKING_HEADCOUNT // MEMORY_HEADCOUNT
    cached_prefix = jnp.take(cached_page_pool, prefix_page_hits.reshape(-1), axis=1).reshape(2, -1, MEMORY_HEADCOUNT * PER_HEAD_DIM)
    owners = jnp.repeat(jnp.arange(R, dtype=jnp.int32), NHIT * PAGE_TOKENS)
    joined_keys = jnp.concatenate([cached_prefix[0], suffix_keys_values[0]], axis=0).reshape(-1, MEMORY_HEADCOUNT, PER_HEAD_DIM).transpose(1, 0, 2)
    joined_values = jnp.concatenate([cached_prefix[1], suffix_keys_values[1]], axis=0).reshape(-1, MEMORY_HEADCOUNT, PER_HEAD_DIM).transpose(1, 0, 2)
    seen_cache = segment[:, None] == owners[None, :]
    seen_suffix = (segment[:, None] == segment[None, :]) & (positions[None, :] <= positions[:, None])
    visible = jnp.concatenate([seen_cache, seen_suffix], axis=1)
    heads = queries.reshape(TAIL_ENTRY_TOTAL, ASKING_HEADCOUNT, PER_HEAD_DIM).transpose(1, 0, 2)
    scale = 1.0 / math.sqrt(PER_HEAD_DIM)

    def one_head(paired):
        head_q, head_idx = paired
        group_idx = head_idx // group_share
        head_k = lax.dynamic_index_in_dim(joined_keys, group_idx, 0, keepdims=False)
        head_v = lax.dynamic_index_in_dim(joined_values, group_idx, 0, keepdims=False)
        scores = jnp.dot(head_q, head_k.T, preferred_element_type=jnp.float32) * scale
        scores = jnp.where(visible, scores, FLOOR_SCORE)
        largest = lax.optimization_barrier(jnp.max(scores, axis=1, keepdims=True))
        weights = jnp.where(visible, jnp.exp(scores - largest), 0.0)
        weight_sum = lax.optimization_barrier(jnp.sum(weights, axis=1, keepdims=True))
        mixed = jnp.dot(weights.astype(jnp.bfloat16), head_v, preferred_element_type=jnp.float32)
        return mixed / weight_sum
    outputs = lax.map(one_head, (heads, jnp.arange(ASKING_HEADCOUNT, dtype=jnp.int32)))
    return outputs.transpose(1, 0, 2).reshape(TAIL_ENTRY_TOTAL, ASKING_HEADCOUNT * PER_HEAD_DIM).astype(jnp.bfloat16)

def mamba_part(mamba_x, gate_z, delta, b_c, a_log, d_skip, state_pool, state_hits, positions, segment, starts):
    rate = -jnp.exp(a_log)
    step_size = jax.nn.softplus(delta.astype(jnp.float32))
    inputs = mamba_x.astype(jnp.float32)
    initial = jnp.take(state_pool, state_hits, axis=0)
    opening = jnp.any(positions[:, None] == starts[None, :], axis=1)

    def advance(carry, pieces):
        step_row, input_row, in_row, out_row, open_flag, seg_idx = pieces
        begun = lax.dynamic_index_in_dim(initial, seg_idx, 0, keepdims=False)
        prior = jnp.where(open_flag, begun, carry)
        decay = jnp.exp(step_row[None, :] * rate)
        fresh = decay * prior + step_row[None, :] * in_row[:, None] * input_row[None, :]
        return (fresh, jnp.dot(out_row, fresh, precision=lax.Precision.HIGHEST))
    start_state = jnp.zeros((NS, STATE_FEATURES), jnp.float32)
    _, outputs = lax.scan(advance, start_state, (step_size, inputs, b_c[0].T, b_c[1].T, opening, segment))
    reply = outputs + d_skip[None, :] * inputs
    return (reply * jax.nn.silu(gate_z.astype(jnp.float32))).astype(jnp.bfloat16)

def reference(queries, suffix_keys_values, cached_page_pool, prefix_page_hits, lengths, mamba_x, gate_z, delta, b_c, a_log, d_skip, state_pool, state_hits):
    positions = jnp.arange(TAIL_ENTRY_TOTAL, dtype=jnp.int32)
    segment, starts = segments_of(positions, lengths)
    attended = attention_part(queries, suffix_keys_values, cached_page_pool, prefix_page_hits, positions, segment)
    mixed = mamba_part(mamba_x, gate_z, delta, b_c, a_log, d_skip, state_pool, state_hits, positions, segment, starts)
    return (attended, mixed)
```

```python
import functools
import math

import jax
import jax.numpy as jnp
from jax import lax
from jax.experimental import pallas as pl
from jax.experimental.pallas import tpu as pltpu
from jax.sharding import PartitionSpec as P

D = 128
LANES = 128
LOG2E = math.log2(math.e)
FLOOR = -1e30
VMEM = pl.BlockSpec(memory_space=pltpu.VMEM)
SMEM = pl.BlockSpec(memory_space=pltpu.SMEM)


def segments_of(positions, lengths):
    ends = jnp.cumsum(lengths)
    starts = ends - lengths
    member = (positions[:, None] >= starts[None, :]).astype(jnp.int32)
    return (jnp.sum(member, axis=1) - 1, starts)


def softplus(v):
    return jnp.maximum(v, 0.0) + jnp.log1p(jnp.exp(-jnp.abs(v)))


def spread_inputs(delta, x, a_log, dt_s, du_s, rate_s):
    tokens, width = delta.shape
    rows = width // LANES
    states = a_log.shape[0]
    for c in range(rows):
        cols = slice(c * LANES, (c + 1) * LANES)
        dt = softplus(delta[:, cols].astype(jnp.float32))
        dt_s[pl.ds(c, tokens, stride=rows), :] = dt
        du_s[pl.ds(c, tokens, stride=rows), :] = dt * x[:, cols].astype(jnp.float32)
        rate_s[pl.ds(c, states, stride=rows), :] = jnp.exp(a_log[:, cols]) * (-LOG2E)


def scan_tokens(tokens, rows, states, dt_s, du_s, rate_s, init_s, b_c, seg, opening, hs, y_s):
    def step(t, carry):
        hs, total = carry
        at = pl.ds(pl.multiple_of(t * rows, 8), rows)
        dt = dt_s[at, :]
        du = du_s[at, :]
        opens = opening[0, t] > 0
        r = seg[0, t]
        new, ys = [], []
        for n in range(states):
            part = slice(n * rows, (n + 1) * rows)
            prior = jnp.where(opens, init_s[r, part, :], hs[n])
            h = jnp.exp2(dt * rate_s[part, :]) * prior + du * b_c[n, t]
            new.append(h)
            if y_s is not None:
                ys.append(h * b_c[states + n, t])
        if y_s is not None:
            while len(ys) > 1:
                ys = [a + b for a, b in zip(ys[::2], ys[1::2])]
            y_s[at, :] = ys[0]
        return (tuple(new), total + dt)

    start = (tuple(hs), jnp.zeros((rows, LANES), jnp.float32))
    return lax.fori_loop(0, tokens, step, start, unroll=2)


def gate_outputs(x, gate, d_skip, y_s, out):
    tokens, width = x.shape
    rows = width // LANES
    for c in range(rows):
        cols = slice(c * LANES, (c + 1) * LANES)
        y = y_s[pl.ds(c, tokens, stride=rows), :]
        v = gate[:, cols].astype(jnp.float32)
        reply = y + d_skip[:, cols] * x[:, cols].astype(jnp.float32)
        out[:, cols] = (reply * (v / (1.0 + jnp.exp(-v)))).astype(out.dtype)


def load_initials(pool, hits, init_s, rows):
    count, states = init_s.shape[0], pool.shape[1]
    for r in range(count):
        chosen = pool[hits[0, r]].astype(jnp.float32)
        for c in range(rows):
            init_s[r, pl.ds(c, states, stride=rows), :] = chosen[:, c * LANES : (c + 1) * LANES]


def last_state_kernel(
    delta, x, a_log, pool, b_c, seg, opening, hits, last, dt_sum, dt_s, du_s, rate_s, init_s
):
    tokens, width = delta.shape
    rows, states = width // LANES, a_log.shape[0]
    spread_inputs(delta, x, a_log, dt_s, du_s, rate_s)
    load_initials(pool, hits, init_s, rows)
    zeros = [jnp.zeros((rows, LANES), jnp.float32)] * states
    hs, total = scan_tokens(
        tokens, rows, states, dt_s, du_s, rate_s, init_s, b_c, seg, opening, zeros, None
    )
    for n in range(states):
        last[n * rows : (n + 1) * rows, :] = hs[n]
    dt_sum[...] = total


def mamba_kernel(
    delta, x, a_log, gate, d_skip, pool, lasts, sums, b_c, seg, opening, hits, opened, place,
    out, dt_s, du_s, rate_s, init_s, y_s, enter_s,
):
    tokens, width = delta.shape
    rows, states = width // LANES, a_log.shape[0]
    spread_inputs(delta, x, a_log, dt_s, du_s, rate_s)
    load_initials(pool, hits, init_s, rows)
    enter_s[...] = jnp.zeros_like(enter_s)

    def join(j, carry):
        kept = jnp.where(opened[0, j] > 0, 0.0, 1.0)
        total = sums[j]
        for n in range(states):
            part = slice(n * rows, (n + 1) * rows)
            decay = jnp.exp2(total * rate_s[part, :]) * kept
            enter_s[part, :] = decay * enter_s[part, :] + lasts[j, part, :].astype(jnp.float32)
        return carry

    lax.fori_loop(0, place[0, 0], join, 0)
    hs = [enter_s[n * rows : (n + 1) * rows, :] for n in range(states)]
    scan_tokens(tokens, rows, states, dt_s, du_s, rate_s, init_s, b_c, seg, opening, hs, y_s)
    gate_outputs(x, gate, d_skip, y_s, out)


def attention_kernel(tile, block, q, suffix, pages, hits, starts, place, out, kept):
    tokens, width = q.shape
    kv_width = suffix.shape[3]
    heads_kv = kv_width // D
    share = width // kv_width
    requests, hit_count = hits.shape
    page_len = pages.shape[3]
    local_pages = pages.shape[2]
    per_shard = suffix.shape[2]
    first = place[0, 0] * tokens
    factor = LOG2E / math.sqrt(D)
    contract_last = (((1,), (1,)), ((), ()))
    rows = share * tile

    for r in range(requests):
        start, end = starts[0, r], starts[0, r + 1]

        @pl.when((start < first + tokens) & (end > first))
        def _():
            for j in range(hit_count):
                page = hits[r, j]
                shard, row = page // local_pages, page % local_pages
                for kind in range(2):
                    kept[kind, j * page_len : (j + 1) * page_len, :] = pages[shard, kind, row]
            for i in range(tokens // tile):
                low = first + i * tile

                @pl.when((start < low + tile) & (end > low))
                def _():
                    token = low + lax.rem(
                        lax.broadcasted_iota(jnp.int32, (rows, 1), 0), jnp.int32(tile)
                    )
                    mine = (token >= start) & (token < end)
                    for g in range(heads_kv):
                        cols = slice(g * D, (g + 1) * D)
                        span = slice(i * tile, (i + 1) * tile)
                        qt = jnp.concatenate(
                            [
                                q[span, (g * share + h) * D : (g * share + h + 1) * D]
                                for h in range(share)
                            ],
                            axis=0,
                        )
                        s = lax.dot_general(
                            qt, kept[0, :, cols], contract_last, preferred_element_type=jnp.float32
                        ) * factor
                        top = jnp.max(s, axis=1, keepdims=True)
                        w = jnp.exp2(s - top)
                        total = jnp.sum(w, axis=1, keepdims=True)
                        acc = jnp.dot(
                            w.astype(jnp.bfloat16),
                            kept[1, :, cols],
                            preferred_element_type=jnp.float32,
                        )

                        def fold(kb, carry):
                            top, total, acc = carry
                            shard = kb // (per_shard // block)
                            off = pl.multiple_of((kb % (per_shard // block)) * block, block)
                            k = suffix[shard, 0, pl.ds(off, block), cols]
                            v = suffix[shard, 1, pl.ds(off, block), cols]
                            key = kb * block + lax.broadcasted_iota(jnp.int32, (1, block), 1)
                            s = lax.dot_general(
                                qt, k, contract_last, preferred_element_type=jnp.float32
                            ) * factor
                            s = jnp.where((key >= start) & (key <= token), s, FLOOR)
                            new = jnp.maximum(top, jnp.max(s, axis=1, keepdims=True))
                            w = jnp.exp2(s - new)
                            shrink = jnp.exp2(top - new)
                            total = total * shrink + jnp.sum(w, axis=1, keepdims=True)
                            acc = acc * shrink + jnp.dot(
                                w.astype(jnp.bfloat16), v, preferred_element_type=jnp.float32
                            )
                            return (new, total, acc)

                        high = jnp.minimum(low + tile, end)
                        top, total, acc = lax.fori_loop(
                            start // block, (high + block - 1) // block, fold, (top, total, acc)
                        )
                        o = acc / total
                        for h in range(share):
                            place_to = slice((g * share + h) * D, (g * share + h + 1) * D)
                            part = slice(h * tile, (h + 1) * tile)
                            out[span, place_to] = jnp.where(
                                mine[part],
                                o[part],
                                out[span, place_to].astype(jnp.float32),
                            ).astype(out.dtype)


def local(
    ctx,
    queries,
    suffix_keys_values,
    cached_page_pool,
    prefix_page_hits,
    lengths,
    mamba_x,
    gate_z,
    delta,
    b_c,
    a_log,
    d_skip,
    state_pool,
    state_hits,
):
    tokens, width = mamba_x.shape
    states = a_log.shape[0]
    rows = width // LANES
    requests = lengths.shape[0]
    me = lax.axis_index("ctx")
    positions = me * tokens + jnp.arange(tokens, dtype=jnp.int32)
    segment, starts = segments_of(positions, lengths)
    opening = jnp.any(positions[:, None] == starts[None, :], axis=1).astype(jnp.int32)
    bounds = jnp.concatenate([starts, starts[-1:] + lengths[-1:]])[None, :]
    holder = starts // tokens
    opened = jnp.any(
        jnp.arange(ctx, dtype=jnp.int32)[:, None] == holder[None, :], axis=1
    ).astype(jnp.int32)[None, :]
    place = jnp.full((1, 1), me, jnp.int32)
    seg, opening = segment[None, :], opening[None, :]
    hits = state_hits[None, :]
    coeffs = b_c.reshape(2 * states, tokens)

    pages = lax.all_gather(cached_page_pool, "ctx")
    suffix = lax.all_gather(suffix_keys_values, "ctx")
    pool = lax.all_gather(state_pool.astype(jnp.bfloat16), "ctx", tiled=True)

    f32 = jnp.float32
    params = pltpu.CompilerParams(vmem_limit_bytes=56 * 1024 * 1024)
    scan_scratch = [
        pltpu.VMEM((tokens * rows, LANES), f32),
        pltpu.VMEM((tokens * rows, LANES), f32),
        pltpu.VMEM((states * rows, LANES), f32),
        pltpu.VMEM((requests, states * rows, LANES), f32),
    ]
    last, total = pl.pallas_call(
        last_state_kernel,
        out_shape=(
            jax.ShapeDtypeStruct((states * rows, LANES), f32),
            jax.ShapeDtypeStruct((rows, LANES), f32),
        ),
        in_specs=[VMEM] * 4 + [SMEM] * 4,
        out_specs=(VMEM, VMEM),
        scratch_shapes=scan_scratch,
        compiler_params=params,
        name="last_state",
    )(delta, mamba_x, a_log, pool, coeffs, seg, opening, hits)
    lasts = lax.all_gather(last.astype(jnp.bfloat16), "ctx")
    sums = lax.all_gather(total, "ctx")

    attended = pl.pallas_call(
        functools.partial(attention_kernel, math.gcd(tokens, 32), math.gcd(tokens, 128)),
        out_shape=jax.ShapeDtypeStruct(queries.shape, queries.dtype),
        in_specs=[VMEM] * 3 + [SMEM] * 3,
        out_specs=VMEM,
        scratch_shapes=[
            pltpu.VMEM(
                (
                    2,
                    prefix_page_hits.shape[1] * cached_page_pool.shape[2],
                    cached_page_pool.shape[3],
                ),
                jnp.bfloat16,
            )
        ],
        compiler_params=params,
        name="attention",
    )(queries, suffix, pages, prefix_page_hits, bounds, place)

    mixed = pl.pallas_call(
        mamba_kernel,
        out_shape=jax.ShapeDtypeStruct(mamba_x.shape, mamba_x.dtype),
        in_specs=[VMEM] * 8 + [SMEM] * 6,
        out_specs=VMEM,
        scratch_shapes=scan_scratch
        + [
            pltpu.VMEM((tokens * rows, LANES), f32),
            pltpu.VMEM((states * rows, LANES), f32),
        ],
        compiler_params=params,
        name="mamba",
    )(
        delta, mamba_x, a_log, gate_z, d_skip[None, :], pool, lasts, sums,
        coeffs, seg, opening, hits, opened, place,
    )
    return (attended, mixed)


def solution(mesh):
    placed = (
        P(("groups", "ctx"), "tp"),
        P(None, ("groups", "ctx"), "tp"),
        P(None, ("groups", "ctx"), None, "tp"),
        P("groups", None),
        P("groups"),
        P(("groups", "ctx"), "tp"),
        P(("groups", "ctx"), "tp"),
        P(("groups", "ctx"), "tp"),
        P(None, None, ("groups", "ctx")),
        P(None, "tp"),
        P("tp"),
        P(("groups", "ctx"), None, "tp"),
        P("groups"),
    )
    return jax.shard_map(
        functools.partial(local, mesh.shape["ctx"]),
        mesh=mesh,
        in_specs=placed,
        out_specs=(P(("groups", "ctx"), "tp"), P(("groups", "ctx"), "tp")),
        check_vma=False,
    )
```

```python
import functools
import math

import jax
import jax.numpy as jnp
from jax import lax
from jax.experimental import pallas as pl
from jax.experimental.pallas import tpu as pltpu
from jax.sharding import PartitionSpec as P

D = 128
LANES = 128
LOG2E = math.log2(math.e)
FLOOR = -1e30
VMEM = pl.BlockSpec(memory_space=pltpu.VMEM)
ANY = pl.BlockSpec(memory_space=pl.ANY)
SMEM = pl.BlockSpec(memory_space=pltpu.SMEM)


def segments_of(positions, lengths):
    ends = jnp.cumsum(lengths)
    starts = ends - lengths
    member = (positions[:, None] >= starts[None, :]).astype(jnp.int32)
    return (jnp.sum(member, axis=1) - 1, starts)


def softplus(v):
    return jnp.maximum(v, 0.0) + jnp.log1p(jnp.exp(-jnp.abs(v)))


def spread_inputs(delta, x, a_log, dt_s, du_s, rate_s):
    tokens, width = delta.shape
    rows = width // LANES
    states = a_log.shape[0]
    for c in range(rows):
        cols = slice(c * LANES, (c + 1) * LANES)
        dt = softplus(delta[:, cols].astype(jnp.float32))
        dt_s[pl.ds(c, tokens, stride=rows), :] = dt
        du_s[pl.ds(c, tokens, stride=rows), :] = dt * x[:, cols].astype(jnp.float32)
        rate_s[pl.ds(c, states, stride=rows), :] = jnp.exp(a_log[:, cols]) * (-LOG2E)


def scan_tokens(tokens, rows, states, dt_s, du_s, rate_s, init_s, b_c, seg, opening, hs, y_s):
    def step(t, carry):
        hs, total = carry
        at = pl.ds(pl.multiple_of(t * rows, 8), rows)
        dt = dt_s[at, :]
        du = du_s[at, :]
        opens = opening[0, t] > 0
        rates = rate_s[...]
        begun = init_s[seg[0, t]]
        new, ys = [], []
        for n in range(states):
            part = slice(n * rows, (n + 1) * rows)
            prior = jnp.where(opens, begun[part], hs[n])
            h = jnp.exp2(dt * rates[part]) * prior + du * b_c[n, t]
            new.append(h)
            if y_s is not None:
                ys.append(h * b_c[states + n, t])
        if y_s is not None:
            while len(ys) > 1:
                ys = [a + b for a, b in zip(ys[::2], ys[1::2])]
            y_s[at, :] = ys[0]
        return (tuple(new), total + dt)

    start = (tuple(hs), jnp.zeros((rows, LANES), jnp.float32))
    return lax.fori_loop(0, tokens, step, start, unroll=2)


def gate_outputs(x, gate, d_skip, y_s, out):
    tokens, width = x.shape
    rows = width // LANES
    for c in range(rows):
        cols = slice(c * LANES, (c + 1) * LANES)
        y = y_s[pl.ds(c, tokens, stride=rows), :]
        v = gate[:, cols].astype(jnp.float32)
        reply = y + d_skip[:, cols] * x[:, cols].astype(jnp.float32)
        out[:, cols] = (reply * (v / (1.0 + jnp.exp(-v)))).astype(out.dtype)


def load_initials(pool, hits, init_s, rows):
    count, states = init_s.shape[0], pool.shape[1]
    for r in range(count):
        chosen = pool[hits[0, r]].astype(jnp.float32)
        for c in range(rows):
            init_s[r, pl.ds(c, states, stride=rows), :] = chosen[:, c * LANES : (c + 1) * LANES]


def exchange_kernel(
    ctx,
    delta, x, a_log, gate, d_skip, pool, b_c, seg, opening, hits, opened, pages, suffix,
    out, pages_all, suffix_all,
    dt_s, du_s, rate_s, init_s, y_s, enter_s, pool_s, mine_s, lasts_s, total_s, totals_s,
    own_sem, page_sem, suffix_sem, pool_sem, last_sem, total_sem,
):
    tokens, width = delta.shape
    rows, states = width // LANES, a_log.shape[0]
    slots = pool.shape[0]
    me = lax.axis_index("ctx")
    peers = range(1, ctx)

    own = [
        pltpu.make_async_copy(pages, pages_all.at[me], own_sem.at[0]),
        pltpu.make_async_copy(suffix, suffix_all.at[me], own_sem.at[1]),
    ]
    for copy in own:
        copy.start()
    held = pl.ds(me * slots, slots)
    pool_s[held] = pool[...].astype(jnp.bfloat16)

    def remote(source, target, sems, d):
        return pltpu.make_async_remote_copy(
            src_ref=source,
            dst_ref=target,
            send_sem=sems.at[0, d - 1],
            recv_sem=sems.at[1, d - 1],
            device_id={"ctx": lax.rem(me + d, ctx)},
            device_id_type=pl.DeviceIdType.MESH,
        )

    barrier = pltpu.get_barrier_semaphore()
    for d in peers:
        pl.semaphore_signal(
            barrier,
            inc=1,
            device_id={"ctx": lax.rem(me + d, ctx)},
            device_id_type=pl.DeviceIdType.MESH,
        )
    pl.semaphore_wait(barrier, ctx - 1)

    pool_copies = [remote(pool_s.at[held], pool_s.at[held], pool_sem, d) for d in peers]
    page_copies = [remote(pages, pages_all.at[me], page_sem, d) for d in peers]
    suffix_copies = [remote(suffix, suffix_all.at[me], suffix_sem, d) for d in peers]
    last_copies = [remote(mine_s, lasts_s.at[d - 1], last_sem, d) for d in peers]
    total_copies = [remote(total_s, totals_s.at[d - 1], total_sem, d) for d in peers]
    for copy in pool_copies:
        copy.start()
    for copy in page_copies:
        copy.start()
    for d in peers:

        @pl.when(me + d < ctx)
        def _():
            suffix_copies[d - 1].start()

    spread_inputs(delta, x, a_log, dt_s, du_s, rate_s)
    for copy in pool_copies:
        copy.wait_recv()
    load_initials(pool_s, hits, init_s, rows)
    zeros = [jnp.zeros((rows, LANES), jnp.float32)] * states
    hs, total = scan_tokens(
        tokens, rows, states, dt_s, du_s, rate_s, init_s, b_c, seg, opening, zeros, None
    )
    mine_s[...] = jnp.concatenate(hs, axis=0).astype(jnp.bfloat16)
    total_s[...] = total
    for d in peers:

        @pl.when(me + d < ctx)
        def _():
            last_copies[d - 1].start()
            total_copies[d - 1].start()

    enter_s[...] = jnp.zeros_like(enter_s)
    for d in reversed(peers):

        @pl.when(me >= d)
        def _():
            last_copies[d - 1].wait_recv()
            total_copies[d - 1].wait_recv()
            kept = jnp.where(opened[0, me - d] > 0, 0.0, 1.0)
            sums = jnp.concatenate([totals_s[d - 1]] * states, axis=0)
            decay = jnp.exp2(sums * rate_s[...]) * kept
            enter_s[...] = decay * enter_s[...] + lasts_s[d - 1].astype(jnp.float32)

    hs = [enter_s[n * rows : (n + 1) * rows, :] for n in range(states)]
    scan_tokens(tokens, rows, states, dt_s, du_s, rate_s, init_s, b_c, seg, opening, hs, y_s)
    gate_outputs(x, gate, d_skip, y_s, out)

    for d in peers:

        @pl.when(me >= d)
        def _():
            suffix_copies[d - 1].wait_recv()

        @pl.when(me + d < ctx)
        def _():
            suffix_copies[d - 1].wait_send()
            last_copies[d - 1].wait_send()
            total_copies[d - 1].wait_send()

        pool_copies[d - 1].wait_send()
        page_copies[d - 1].wait()
    for copy in own:
        copy.wait()


def attention_kernel(tile, block, q, suffix, pages, hits, starts, place, out, kept):
    tokens, width = q.shape
    kv_width = suffix.shape[3]
    heads_kv = kv_width // D
    share = width // kv_width
    requests, hit_count = hits.shape
    page_len = pages.shape[3]
    local_pages = pages.shape[2]
    per_shard = suffix.shape[2]
    first = place[0, 0] * tokens
    factor = LOG2E / math.sqrt(D)
    contract_last = (((1,), (1,)), ((), ()))
    rows = share * tile

    for r in range(requests):
        start, end = starts[0, r], starts[0, r + 1]

        @pl.when((start < first + tokens) & (end > first))
        def _():
            for j in range(hit_count):
                page = hits[r, j]
                shard, row = page // local_pages, page % local_pages
                for kind in range(2):
                    kept[kind, j * page_len : (j + 1) * page_len, :] = pages[shard, kind, row]
            for i in range(tokens // tile):
                low = first + i * tile

                @pl.when((start < low + tile) & (end > low))
                def _():
                    token = low + lax.rem(
                        lax.broadcasted_iota(jnp.int32, (rows, 1), 0), jnp.int32(tile)
                    )
                    mine = (token >= start) & (token < end)
                    for g in range(heads_kv):
                        cols = slice(g * D, (g + 1) * D)
                        span = slice(i * tile, (i + 1) * tile)
                        qt = jnp.concatenate(
                            [
                                q[span, (g * share + h) * D : (g * share + h + 1) * D]
                                for h in range(share)
                            ],
                            axis=0,
                        )
                        s = lax.dot_general(
                            qt, kept[0, :, cols], contract_last, preferred_element_type=jnp.float32
                        ) * factor
                        top = jnp.max(s, axis=1, keepdims=True)
                        w = jnp.exp2(s - top)
                        total = jnp.sum(w, axis=1, keepdims=True)
                        acc = jnp.dot(
                            w.astype(jnp.bfloat16),
                            kept[1, :, cols],
                            preferred_element_type=jnp.float32,
                        )

                        def fold(kb, carry):
                            top, total, acc = carry
                            shard = kb // (per_shard // block)
                            off = pl.multiple_of((kb % (per_shard // block)) * block, block)
                            k = suffix[shard, 0, pl.ds(off, block), cols]
                            v = suffix[shard, 1, pl.ds(off, block), cols]
                            key = kb * block + lax.broadcasted_iota(jnp.int32, (1, block), 1)
                            s = lax.dot_general(
                                qt, k, contract_last, preferred_element_type=jnp.float32
                            ) * factor
                            s = jnp.where((key >= start) & (key <= token), s, FLOOR)
                            new = jnp.maximum(top, jnp.max(s, axis=1, keepdims=True))
                            w = jnp.exp2(s - new)
                            shrink = jnp.exp2(top - new)
                            total = total * shrink + jnp.sum(w, axis=1, keepdims=True)
                            acc = acc * shrink + jnp.dot(
                                w.astype(jnp.bfloat16), v, preferred_element_type=jnp.float32
                            )
                            return (new, total, acc)

                        high = jnp.minimum(low + tile, end)
                        top, total, acc = lax.fori_loop(
                            start // block, (high + block - 1) // block, fold, (top, total, acc)
                        )
                        o = acc / total
                        for h in range(share):
                            place_to = slice((g * share + h) * D, (g * share + h + 1) * D)
                            part = slice(h * tile, (h + 1) * tile)
                            out[span, place_to] = jnp.where(
                                mine[part],
                                o[part],
                                out[span, place_to].astype(jnp.float32),
                            ).astype(out.dtype)


def local(
    ctx,
    queries,
    suffix_keys_values,
    cached_page_pool,
    prefix_page_hits,
    lengths,
    mamba_x,
    gate_z,
    delta,
    b_c,
    a_log,
    d_skip,
    state_pool,
    state_hits,
):
    tokens, width = mamba_x.shape
    states = a_log.shape[0]
    rows = width // LANES
    requests = lengths.shape[0]
    me = lax.axis_index("ctx")
    positions = me * tokens + jnp.arange(tokens, dtype=jnp.int32)
    segment, starts = segments_of(positions, lengths)
    opening = jnp.any(positions[:, None] == starts[None, :], axis=1).astype(jnp.int32)
    bounds = jnp.concatenate([starts, starts[-1:] + lengths[-1:]])[None, :]
    holder = starts // tokens
    opened = jnp.any(
        jnp.arange(ctx, dtype=jnp.int32)[:, None] == holder[None, :], axis=1
    ).astype(jnp.int32)[None, :]
    place = jnp.full((1, 1), me, jnp.int32)
    seg, opening = segment[None, :], opening[None, :]
    hits = state_hits[None, :]
    coeffs = b_c.reshape(2 * states, tokens)

    f32, bf16 = jnp.float32, jnp.bfloat16
    params = pltpu.CompilerParams(vmem_limit_bytes=56 * 1024 * 1024)
    slots = state_pool.shape[0]
    sems = pltpu.SemaphoreType.DMA((2, ctx - 1))
    whole = pltpu.VMEM((tokens * rows, LANES), f32)
    state = pltpu.VMEM((states * rows, LANES), f32)
    mixed, pages, suffix = pl.pallas_call(
        functools.partial(exchange_kernel, ctx),
        out_shape=(
            jax.ShapeDtypeStruct(mamba_x.shape, mamba_x.dtype),
            jax.ShapeDtypeStruct((ctx,) + cached_page_pool.shape, bf16),
            jax.ShapeDtypeStruct((ctx,) + suffix_keys_values.shape, bf16),
        ),
        in_specs=[VMEM] * 6 + [SMEM] * 5 + [ANY] * 2,
        out_specs=(VMEM, ANY, ANY),
        scratch_shapes=[
            whole,
            whole,
            state,
            pltpu.VMEM((requests, states * rows, LANES), f32),
            whole,
            state,
            pltpu.VMEM((ctx * slots, states, width), bf16),
            pltpu.VMEM((states * rows, LANES), bf16),
            pltpu.VMEM((ctx - 1, states * rows, LANES), bf16),
            pltpu.VMEM((rows, LANES), f32),
            pltpu.VMEM((ctx - 1, rows, LANES), f32),
            pltpu.SemaphoreType.DMA((2,)),
            sems,
            sems,
            sems,
            sems,
            sems,
        ],
        compiler_params=pltpu.CompilerParams(
            collective_id=0, has_side_effects=True, vmem_limit_bytes=56 * 1024 * 1024
        ),
        name="exchange_and_mamba",
    )(
        delta, mamba_x, a_log, gate_z, d_skip[None, :], state_pool,
        coeffs, seg, opening, hits, opened, cached_page_pool, suffix_keys_values,
    )

    attended = pl.pallas_call(
        functools.partial(attention_kernel, math.gcd(tokens, 32), math.gcd(tokens, 128)),
        out_shape=jax.ShapeDtypeStruct(queries.shape, queries.dtype),
        in_specs=[VMEM] * 3 + [SMEM] * 3,
        out_specs=VMEM,
        scratch_shapes=[
            pltpu.VMEM(
                (
                    2,
                    prefix_page_hits.shape[1] * cached_page_pool.shape[2],
                    cached_page_pool.shape[3],
                ),
                jnp.bfloat16,
            )
        ],
        compiler_params=params,
        name="attention",
    )(queries, suffix, pages, prefix_page_hits, bounds, place)

    return (attended, mixed)


def solution(mesh):
    placed = (
        P(("groups", "ctx"), "tp"),
        P(None, ("groups", "ctx"), "tp"),
        P(None, ("groups", "ctx"), None, "tp"),
        P("groups", None),
        P("groups"),
        P(("groups", "ctx"), "tp"),
        P(("groups", "ctx"), "tp"),
        P(("groups", "ctx"), "tp"),
        P(None, None, ("groups", "ctx")),
        P(None, "tp"),
        P("tp"),
        P(("groups", "ctx"), None, "tp"),
        P("groups"),
    )
    return jax.shard_map(
        functools.partial(local, mesh.shape["ctx"]),
        mesh=mesh,
        in_specs=placed,
        out_specs=(P(("groups", "ctx"), "tp"), P(("groups", "ctx"), "tp")),
        check_vma=False,
    )
```

```python
import functools
import math

import jax
import jax.numpy as jnp
from jax import lax
from jax.experimental import pallas as pl
from jax.experimental.pallas import tpu as pltpu
from jax.sharding import PartitionSpec as P

D = 128
LANES = 128
LOG2E = math.log2(math.e)
FLOOR = -1e30
VMEM = pl.BlockSpec(memory_space=pltpu.VMEM)
ANY = pl.BlockSpec(memory_space=pl.ANY)
SMEM = pl.BlockSpec(memory_space=pltpu.SMEM)


def segments_of(positions, lengths):
    order = jnp.arange(lengths.shape[0], dtype=jnp.int32)
    earlier = order[None, :] < order[:, None]
    starts = jnp.sum(jnp.where(earlier, lengths[None, :], 0), axis=1)
    member = (positions[:, None] >= starts[None, :]).astype(jnp.int32)
    return (jnp.sum(member, axis=1) - 1, starts)


def softplus(v):
    return jnp.maximum(v, 0.0) + jnp.log1p(jnp.exp(-jnp.abs(v)))


def spread_inputs(delta, x, a_log, dt_s, du_s, rate_s):
    tokens, width = delta.shape
    rows = width // LANES
    states = a_log.shape[0]
    for c in range(rows):
        cols = slice(c * LANES, (c + 1) * LANES)
        dt = softplus(delta[:, cols].astype(jnp.float32))
        dt_s[pl.ds(c, tokens, stride=rows), :] = dt
        du_s[pl.ds(c, tokens, stride=rows), :] = dt * x[:, cols].astype(jnp.float32)
        rate_s[pl.ds(c, states, stride=rows), :] = jnp.exp(a_log[:, cols]) * (-LOG2E)


def scan_tokens(tokens, rows, states, dt_s, du_s, rate_s, init_s, b_c, seg, opening, hs, y_s):
    def step(t, carry):
        hs, total = carry
        at = pl.ds(pl.multiple_of(t * rows, 8), rows)
        dt = dt_s[at, :]
        du = du_s[at, :]
        opens = opening[0, t] > 0
        rates = rate_s[...]
        begun = init_s[seg[0, t]]
        new, ys = [], []
        for n in range(states):
            part = slice(n * rows, (n + 1) * rows)
            prior = jnp.where(opens, begun[part], hs[n])
            h = jnp.exp2(dt * rates[part]) * prior + du * b_c[n, t]
            new.append(h)
            if y_s is not None:
                ys.append(h * b_c[states + n, t])
        if y_s is not None:
            while len(ys) > 1:
                ys = [a + b for a, b in zip(ys[::2], ys[1::2])]
            y_s[at, :] = ys[0]
        return (tuple(new), total + dt)

    start = (tuple(hs), jnp.zeros((rows, LANES), jnp.float32))
    return lax.fori_loop(0, tokens, step, start, unroll=2)


def gate_outputs(x, gate, d_skip, y_s, out):
    tokens, width = x.shape
    rows = width // LANES
    for c in range(rows):
        cols = slice(c * LANES, (c + 1) * LANES)
        y = y_s[pl.ds(c, tokens, stride=rows), :]
        v = gate[:, cols].astype(jnp.float32)
        reply = y + d_skip[:, cols] * x[:, cols].astype(jnp.float32)
        out[:, cols] = (reply * (v / (1.0 + jnp.exp(-v)))).astype(out.dtype)


def load_initials(pool, hits, init_s, rows):
    count, states = init_s.shape[0], pool.shape[1]
    for r in range(count):
        chosen = pool[hits[0, r]].astype(jnp.float32)
        for c in range(rows):
            init_s[r, pl.ds(c, states, stride=rows), :] = chosen[:, c * LANES : (c + 1) * LANES]


def exchange_kernel(
    ctx,
    delta, x, a_log, gate, d_skip, pool, b_c, seg, opening, hits, opened, pages, suffix,
    out, pages_all, suffix_all,
    dt_s, du_s, rate_s, init_s, y_s, enter_s, pool_s, mine_s, lasts_s, total_s, totals_s,
    own_sem, page_sem, suffix_sem, pool_sem, last_sem, total_sem,
):
    tokens, width = delta.shape
    rows, states = width // LANES, a_log.shape[0]
    slots = pool.shape[0]
    me = lax.axis_index("ctx")
    peers = range(1, ctx)

    own = [
        pltpu.make_async_copy(pages, pages_all.at[me], own_sem.at[0]),
        pltpu.make_async_copy(suffix, suffix_all.at[me], own_sem.at[1]),
    ]
    for copy in own:
        copy.start()
    held = pl.ds(me * slots, slots)
    pool_s[held] = pool[...].astype(jnp.bfloat16)

    def remote(source, target, sems, d):
        return pltpu.make_async_remote_copy(
            src_ref=source,
            dst_ref=target,
            send_sem=sems.at[0, d - 1],
            recv_sem=sems.at[1, d - 1],
            device_id={"ctx": lax.rem(me + d, ctx)},
            device_id_type=pl.DeviceIdType.MESH,
        )

    barrier = pltpu.get_barrier_semaphore()
    for d in peers:
        pl.semaphore_signal(
            barrier,
            inc=1,
            device_id={"ctx": lax.rem(me + d, ctx)},
            device_id_type=pl.DeviceIdType.MESH,
        )
    pl.semaphore_wait(barrier, ctx - 1)

    pool_copies = [remote(pool_s.at[held], pool_s.at[held], pool_sem, d) for d in peers]

    def hop(way, step, half, shard):
        source = pages.at[half] if step == 1 else pages_all.at[shard, half]
        return pltpu.make_async_remote_copy(
            src_ref=source,
            dst_ref=pages_all.at[shard, half],
            send_sem=page_sem.at[0, way, half, step - 1],
            recv_sem=page_sem.at[1, way, half, step - 1],
            device_id={"ctx": lax.rem(me + (1 if way == 0 else ctx - 1), ctx)},
            device_id_type=pl.DeviceIdType.MESH,
        )

    def sends(way, step):
        if way == 0:
            return me - (step - 1), (me + 1 < ctx) & (me - (step - 1) >= 0)
        return me + (step - 1), (me >= 1) & (me + (step - 1) < ctx)

    def begin(step, half):
        for way in range(2):
            shard, valid = sends(way, step)

            @pl.when(valid)
            def _():
                hop(way, step, half, shard).start()

    def advance(step):
        for half in range(2):
            for way in range(2):
                shard = me - step if way == 0 else me + step

                @pl.when((shard >= 0) & (shard < ctx))
                def _():
                    hop(way, step, half, shard).wait_recv()

            if step + 1 < ctx:
                begin(step + 1, half)

    suffix_copies = [remote(suffix, suffix_all.at[me], suffix_sem, d) for d in peers]
    last_copies = [remote(mine_s, lasts_s.at[d - 1], last_sem, d) for d in peers]
    total_copies = [remote(total_s, totals_s.at[d - 1], total_sem, d) for d in peers]
    for copy in pool_copies:
        copy.start()
    if ctx > 1:
        for half in range(2):
            begin(1, half)
    for d in peers:

        @pl.when(me + d < ctx)
        def _():
            suffix_copies[d - 1].start()

    spread_inputs(delta, x, a_log, dt_s, du_s, rate_s)
    for copy in pool_copies:
        copy.wait_recv()
    load_initials(pool_s, hits, init_s, rows)
    zeros = [jnp.zeros((rows, LANES), jnp.float32)] * states
    hs, total = scan_tokens(
        tokens, rows, states, dt_s, du_s, rate_s, init_s, b_c, seg, opening, zeros, None
    )
    mine_s[...] = jnp.concatenate(hs, axis=0).astype(jnp.bfloat16)
    total_s[...] = total
    for d in peers:

        @pl.when(me + d < ctx)
        def _():
            last_copies[d - 1].start()
            total_copies[d - 1].start()

    if ctx > 1:
        advance(1)
    enter_s[...] = jnp.zeros_like(enter_s)
    for d in reversed(peers):

        @pl.when(me >= d)
        def _():
            last_copies[d - 1].wait_recv()
            total_copies[d - 1].wait_recv()
            kept = jnp.where(opened[0, me - d] > 0, 0.0, 1.0)
            sums = jnp.concatenate([totals_s[d - 1]] * states, axis=0)
            decay = jnp.exp2(sums * rate_s[...]) * kept
            enter_s[...] = decay * enter_s[...] + lasts_s[d - 1].astype(jnp.float32)

    hs = [enter_s[n * rows : (n + 1) * rows, :] for n in range(states)]
    scan_tokens(tokens, rows, states, dt_s, du_s, rate_s, init_s, b_c, seg, opening, hs, y_s)
    if ctx > 2:
        advance(2)
    gate_outputs(x, gate, d_skip, y_s, out)
    for step in range(3, ctx):
        advance(step)

    for step in peers:
        for way in range(2):
            shard, valid = sends(way, step)

            @pl.when(valid)
            def _():
                for half in range(2):
                    hop(way, step, half, shard).wait_send()

    for d in peers:

        @pl.when(me >= d)
        def _():
            suffix_copies[d - 1].wait_recv()

        @pl.when(me + d < ctx)
        def _():
            suffix_copies[d - 1].wait_send()
            last_copies[d - 1].wait_send()
            total_copies[d - 1].wait_send()

        pool_copies[d - 1].wait_send()
    for copy in own:
        copy.wait()


def attention_kernel(tile, block, q, suffix, pages, hits, starts, place, out, kept):
    tokens, width = q.shape
    kv_width = suffix.shape[3]
    heads_kv = kv_width // D
    share = width // kv_width
    requests, hit_count = hits.shape
    page_len = pages.shape[3]
    local_pages = pages.shape[2]
    per_shard = suffix.shape[2]
    first = place[0, 0] * tokens
    factor = LOG2E / math.sqrt(D)
    contract_last = (((1,), (1,)), ((), ()))
    rows = share * tile

    for r in range(requests):
        start, end = starts[0, r], starts[0, r + 1]

        @pl.when((start < first + tokens) & (end > first))
        def _():
            for j in range(hit_count):
                page = hits[r, j]
                shard, row = page // local_pages, page % local_pages
                for kind in range(2):
                    kept[kind, j * page_len : (j + 1) * page_len, :] = pages[shard, kind, row]
            for i in range(tokens // tile):
                low = first + i * tile

                @pl.when((start < low + tile) & (end > low))
                def _():
                    token = low + lax.rem(
                        lax.broadcasted_iota(jnp.int32, (rows, 1), 0), jnp.int32(tile)
                    )
                    mine = (token >= start) & (token < end)
                    for g in range(heads_kv):
                        cols = slice(g * D, (g + 1) * D)
                        span = slice(i * tile, (i + 1) * tile)
                        qt = jnp.concatenate(
                            [
                                q[span, (g * share + h) * D : (g * share + h + 1) * D]
                                for h in range(share)
                            ],
                            axis=0,
                        )
                        s = lax.dot_general(
                            qt, kept[0, :, cols], contract_last, preferred_element_type=jnp.float32
                        ) * factor
                        top = jnp.max(s, axis=1, keepdims=True)
                        w = jnp.exp2(s - top)
                        total = jnp.sum(w, axis=1, keepdims=True)
                        acc = jnp.dot(
                            w.astype(jnp.bfloat16),
                            kept[1, :, cols],
                            preferred_element_type=jnp.float32,
                        )

                        def fold(kb, carry):
                            top, total, acc = carry
                            shard = kb // (per_shard // block)
                            off = pl.multiple_of((kb % (per_shard // block)) * block, block)
                            k = suffix[shard, 0, pl.ds(off, block), cols]
                            v = suffix[shard, 1, pl.ds(off, block), cols]
                            key = kb * block + lax.broadcasted_iota(jnp.int32, (1, block), 1)
                            s = lax.dot_general(
                                qt, k, contract_last, preferred_element_type=jnp.float32
                            ) * factor
                            s = jnp.where((key >= start) & (key <= token), s, FLOOR)
                            new = jnp.maximum(top, jnp.max(s, axis=1, keepdims=True))
                            w = jnp.exp2(s - new)
                            shrink = jnp.exp2(top - new)
                            total = total * shrink + jnp.sum(w, axis=1, keepdims=True)
                            acc = acc * shrink + jnp.dot(
                                w.astype(jnp.bfloat16), v, preferred_element_type=jnp.float32
                            )
                            return (new, total, acc)

                        high = jnp.minimum(low + tile, end)
                        top, total, acc = lax.fori_loop(
                            start // block, (high + block - 1) // block, fold, (top, total, acc)
                        )
                        o = acc / total
                        for h in range(share):
                            place_to = slice((g * share + h) * D, (g * share + h + 1) * D)
                            part = slice(h * tile, (h + 1) * tile)
                            out[span, place_to] = jnp.where(
                                mine[part],
                                o[part],
                                out[span, place_to].astype(jnp.float32),
                            ).astype(out.dtype)


def local(
    ctx,
    queries,
    suffix_keys_values,
    cached_page_pool,
    prefix_page_hits,
    lengths,
    mamba_x,
    gate_z,
    delta,
    b_c,
    a_log,
    d_skip,
    state_pool,
    state_hits,
):
    tokens, width = mamba_x.shape
    states = a_log.shape[0]
    rows = width // LANES
    requests = lengths.shape[0]
    me = lax.axis_index("ctx")
    positions = me * tokens + jnp.arange(tokens, dtype=jnp.int32)
    segment, starts = segments_of(positions, lengths)
    opening = jnp.any(positions[:, None] == starts[None, :], axis=1).astype(jnp.int32)
    bounds = jnp.concatenate([starts, starts[-1:] + lengths[-1:]])[None, :]
    holder = starts // tokens
    opened = jnp.any(
        jnp.arange(ctx, dtype=jnp.int32)[:, None] == holder[None, :], axis=1
    ).astype(jnp.int32)[None, :]
    place = jnp.full((1, 1), me, jnp.int32)
    seg, opening = segment[None, :], opening[None, :]
    hits = state_hits[None, :]
    coeffs = b_c.reshape(2 * states, tokens)

    f32, bf16 = jnp.float32, jnp.bfloat16
    params = pltpu.CompilerParams(vmem_limit_bytes=56 * 1024 * 1024)
    slots = state_pool.shape[0]
    sems = pltpu.SemaphoreType.DMA((2, ctx - 1))
    whole = pltpu.VMEM((tokens * rows, LANES), f32)
    state = pltpu.VMEM((states * rows, LANES), f32)
    mixed, pages, suffix = pl.pallas_call(
        functools.partial(exchange_kernel, ctx),
        out_shape=(
            jax.ShapeDtypeStruct(mamba_x.shape, mamba_x.dtype),
            jax.ShapeDtypeStruct((ctx,) + cached_page_pool.shape, bf16),
            jax.ShapeDtypeStruct((ctx,) + suffix_keys_values.shape, bf16),
        ),
        in_specs=[VMEM] * 6 + [SMEM] * 5 + [ANY] * 2,
        out_specs=(VMEM, ANY, ANY),
        scratch_shapes=[
            whole,
            whole,
            state,
            pltpu.VMEM((requests, states * rows, LANES), f32),
            whole,
            state,
            pltpu.VMEM((ctx * slots, states, width), bf16),
            pltpu.VMEM((states * rows, LANES), bf16),
            pltpu.VMEM((ctx - 1, states * rows, LANES), bf16),
            pltpu.VMEM((rows, LANES), f32),
            pltpu.VMEM((ctx - 1, rows, LANES), f32),
            pltpu.SemaphoreType.DMA((2,)),
            pltpu.SemaphoreType.DMA((2, 2, 2, ctx - 1)),
            sems,
            sems,
            sems,
            sems,
        ],
        compiler_params=pltpu.CompilerParams(
            collective_id=0, has_side_effects=True, vmem_limit_bytes=56 * 1024 * 1024
        ),
        name="exchange_and_mamba",
    )(
        delta, mamba_x, a_log, gate_z, d_skip[None, :], state_pool,
        coeffs, seg, opening, hits, opened, cached_page_pool, suffix_keys_values,
    )

    attended = pl.pallas_call(
        functools.partial(attention_kernel, math.gcd(tokens, 32), math.gcd(tokens, 128)),
        out_shape=jax.ShapeDtypeStruct(queries.shape, queries.dtype),
        in_specs=[VMEM] * 3 + [SMEM] * 3,
        out_specs=VMEM,
        scratch_shapes=[
            pltpu.VMEM(
                (
                    2,
                    prefix_page_hits.shape[1] * cached_page_pool.shape[2],
                    cached_page_pool.shape[3],
                ),
                jnp.bfloat16,
            )
        ],
        compiler_params=params,
        name="attention",
    )(queries, suffix, pages, prefix_page_hits, bounds, place)

    return (attended, mixed)


def solution(mesh):
    placed = (
        P(("groups", "ctx"), "tp"),
        P(None, ("groups", "ctx"), "tp"),
        P(None, ("groups", "ctx"), None, "tp"),
        P("groups", None),
        P("groups"),
        P(("groups", "ctx"), "tp"),
        P(("groups", "ctx"), "tp"),
        P(("groups", "ctx"), "tp"),
        P(None, None, ("groups", "ctx")),
        P(None, "tp"),
        P("tp"),
        P(("groups", "ctx"), None, "tp"),
        P("groups"),
    )
    return jax.shard_map(
        functools.partial(local, mesh.shape["ctx"]),
        mesh=mesh,
        in_specs=placed,
        out_specs=(P(("groups", "ctx"), "tp"), P(("groups", "ctx"), "tp")),
        check_vma=False,
    )
```
